32 devices in a mesh: fsdp: 8 (over z, y), seq: 4 (over x, core).
Axes of the slice: x: 2, y: 2, z: 4, core: 2. Of those that a mesh axis runs over, the one named last changes fastest.
Arguments:
- hidden_in: bfloat16 [4096, 768], P(('fsdp', 'seq')), may hold values from -6 to 6
- cu_lengths: int32 [8, 7], P('fsdp'), may hold values from 0 to 512, as said below
- w_qkv: bfloat16 [2, 768, 2304], P(None, 'fsdp'), may hold values from -0.21875 to 0.21875
- w_attn_out: bfloat16 [2, 768, 768], P(None, 'fsdp'), may hold values from -0.875 to 0.875
- w_in: bfloat16 [2, 768, 2304], P(None, 'fsdp'), may hold values from -0.21875 to 0.21875
- w_ff_out: bfloat16 [2, 1152, 768], P(None, 'fsdp'), may hold values from -0.1875 to 0.1875
- gains: bfloat16 [2, 2, 768], P(None, None, 'fsdp'), may hold values from 0.25 to 1.75
- cotangent: bfloat16 [4096, 768], P(('fsdp', 'seq')), may hold values from -6 to 6
Outputs:
- block_out: bfloat16 [4096, 768], P(('fsdp', 'seq'))
- grad_hidden: float32 [4096, 768], P(('fsdp', 'seq'))
- grad_w_qkv: float32 [2, 768, 2304], P(None, 'fsdp')
- grad_w_attn_out: float32 [2, 768, 768], P(None, 'fsdp')
- grad_w_in: float32 [2, 768, 2304], P(None, 'fsdp')
- grad_w_ff_out: float32 [2, 1152, 768], P(None, 'fsdp')
- grad_gains: float32 [2, 2, 768], P(None, None, 'fsdp')
The draws below stay inside these ranges and needn't reach their ends.
Inputs may be any that keep to these rules, and one draw needn't show every extreme that they name: `cu_lengths`: in every group the entries rise strictly from 0 to 512; one document starts before token 128 and ends after token 384.
All inputs are finite; a program needn't handle non-finite values.
Results may differ from the reference program's by a relative error of at most 0.025.
Values may be sent and summed in bfloat16 or wider, within the bound.
A program may use at most 192 MiB of HBM per device.

```python
import jax
import jax.numpy as jnp
from jax import lax

D = 768
HEADS = 12
HEAD = 64
FF = 1152
LAYERS = 2
HALF_WINDOW = 64
DOCS = 6
TOK_DEV = 128
GROUP_TOK = 512
GROUPS = 8
TOKENS = 4096


def one_pack(key):
    key_long, key_lower, key_upper = jax.random.split(key, 3)
    longest = jax.random.randint(key_long, (), 0, DOCS)
    lower_pool = jax.random.permutation(key_lower, jnp.arange(1, TOK_DEV, dtype=jnp.int32))[:DOCS - 1]
    upper_pool = jax.random.permutation(key_upper, jnp.arange(GROUP_TOK - TOK_DEV + 1, GROUP_TOK, dtype=jnp.int32))[:DOCS - 1]
    lower_pool = jnp.sort(lower_pool)
    upper_pool = jnp.sort(upper_pool)
    index_row = jnp.arange(DOCS - 1, dtype=jnp.int32)
    cuts = jnp.where(index_row < longest, lower_pool, upper_pool)
    first = jnp.zeros((1,), jnp.int32)
    final = jnp.full((1,), GROUP_TOK, jnp.int32)
    return jnp.concatenate([first, cuts.astype(jnp.int32), final]).astype(jnp.int32)


def draw_cu_lengths(key, part):
    key = jax.random.fold_in(key, 7)
    keys_all = jax.random.split(key, GROUPS)
    return jax.vmap(one_pack)(keys_all)


def shard_levels(own_key, shape, cuts, low, high):
    def one(axis_at, blocks):
        draws = jax.random.uniform(jax.random.fold_in(jax.random.fold_in(own_key, 6), axis_at), (blocks,), jnp.float32, low / len(cuts), high / len(cuts))
        return jnp.repeat(jnp.exp(draws), shape[axis_at] // blocks).reshape((-1,) + (1,) * (len(shape) - axis_at - 1))

    level = one(*cuts[0])
    for cut in cuts[1:]:
        level = level * one(*cut)
    return level


def scatter_about(stream_key, dims, scale, most, cuts=(), kind=jnp.bfloat16):
    array = scale * jax.random.normal(stream_key, dims, jnp.float32)
    if cuts:
        array = array * shard_levels(stream_key, dims, cuts, -0.22, 0.18)
    return jnp.clip(array, -most, most).astype(kind)


def setup_inputs(seed: int = 0) -> dict:
    keys = jax.random.split(jax.random.key(seed), 9)
    hidden_in = scatter_about(keys[0], (TOKENS, D), 1.0, 6.0, ((0, 32),))
    cu_lengths = draw_cu_lengths(jax.random.fold_in(keys[8], 71), 0)
    w_qkv = scatter_about(keys[2], (LAYERS, D, 3 * D), D ** -0.5, 0.21875, ((1, 8),))
    w_attn_out = scatter_about(keys[3], (LAYERS, D, D), (D // 16) ** -0.5, 0.875, ((1, 8),))
    w_in = scatter_about(keys[4], (LAYERS, D, 2 * FF), D ** -0.5, 0.21875, ((1, 8),))
    w_ff_out = scatter_about(keys[5], (LAYERS, FF, D), FF ** -0.5, 0.1875, ((1, 8),))
    gains = jnp.clip(1.0 + 0.15 * jax.random.normal(keys[6], (LAYERS, 2, D), jnp.float32), 0.25, 1.75).astype(jnp.bfloat16)
    cotangent = scatter_about(keys[7], (TOKENS, D), 1.0, 6.0, ((0, 32),))
    return dict(hidden_in=hidden_in, cu_lengths=cu_lengths, w_qkv=w_qkv, w_attn_out=w_attn_out, w_in=w_in, w_ff_out=w_ff_out, gains=gains, cotangent=cotangent)


EPS = 1e-05
NEG = -1e+30
LOCAL_BASE = 10000.0
GLOBAL_BASE = 160000.0
HIGH = lax.Precision.HIGHEST

@jax.custom_vjp
def low(v):
    return lax.optimization_barrier(v.astype(jnp.bfloat16)).astype(jnp.float32)

@jax.custom_vjp
def low_back(v):
    return v

def low_keep(v):
    return (low(v), None)

def low_pass(kept, grad):
    return (grad,)

def back_keep(v):
    return (v, None)

def back_low(kept, grad):
    return (low(grad),)
low.defvjp(low_keep, low_pass)
low_back.defvjp(back_keep, back_low)

def layer_norm(stream, gain):
    mean_row = lax.optimization_barrier(jnp.mean(stream, axis=-1, keepdims=True))
    centred = stream - mean_row
    spread = lax.optimization_barrier(jnp.mean(centred * centred, axis=-1, keepdims=True))
    return centred * lax.rsqrt(spread + EPS) * gain

def doc_layout(cu_row):
    places = jnp.arange(GROUP_TOK, dtype=jnp.int32)
    inner_cuts = cu_row[1:DOCS]
    doc_ids = lax.optimization_barrier(jnp.sum((places[:, None] >= inner_cuts[None, :]).astype(jnp.int32), axis=1))
    heads_of = cu_row[:DOCS]
    starts = lax.optimization_barrier(jnp.max(jnp.where(places[:, None] >= heads_of[None, :], heads_of[None, :], 0), axis=1))
    return (doc_ids, places - starts)

def rope_tables(positions, base_freq):
    freqs = base_freq ** (-jnp.arange(0, HEAD, 2, dtype=jnp.float32) / HEAD)
    angles = positions.astype(jnp.float32)[:, None] * freqs[None, :]
    angles = jnp.concatenate([angles, angles], axis=1)
    return (jnp.cos(angles), jnp.sin(angles))

def rotate(values, cosine, sine_tab):
    half_width = values.shape[-1] // 2
    turned = jnp.concatenate([-values[..., half_width:], values[..., :half_width]], axis=-1)
    return values * cosine[:, None, :] + turned * sine_tab[:, None, :]

def attention(queries, key_rows, values, doc_all, reach):
    score_scale = HEAD ** (-0.5)

    def one_group(pieces):
        group_q, group_k, group_v, doc_ids = pieces
        places = jnp.arange(GROUP_TOK, dtype=jnp.int32)
        distance = jnp.abs(places[:, None] - places[None, :])
        allowed = (doc_ids[:, None] == doc_ids[None, :]) & (distance <= reach)
        scores = jnp.einsum('qhd,khd->hqk', group_q, group_k, precision=HIGH) * score_scale
        scores = low_back(scores)
        scores = jnp.where(allowed[None], scores, NEG)
        row_max = lax.optimization_barrier(jnp.max(scores, axis=-1, keepdims=True))
        expd = jnp.exp(scores - row_max)
        attn_probs = low(expd / lax.optimization_barrier(jnp.sum(expd, axis=-1, keepdims=True)))
        return jnp.einsum('hqk,khd->qhd', attn_probs, group_v, precision=HIGH)
    shape_g = (GROUPS, GROUP_TOK, HEADS, HEAD)
    result = lax.map(jax.checkpoint(one_group), (queries.reshape(shape_g), key_rows.reshape(shape_g), values.reshape(shape_g), doc_all))
    return result.reshape(TOKENS, HEADS, HEAD)

def forward(stream, w_qkv, w_attn_out, w_in, w_ff_out, gains, cu_lengths):
    doc_all, positions = jax.vmap(doc_layout)(cu_lengths)
    flat_pos = positions.reshape(-1)
    for layer_at in range(LAYERS):
        reach = HALF_WINDOW if layer_at == 0 else GROUP_TOK
        base_freq = LOCAL_BASE if layer_at == 0 else GLOBAL_BASE
        cosine, sine_tab = rope_tables(flat_pos, base_freq)
        normed = low(layer_norm(stream, gains[layer_at, 0]))
        qkv_rows = low_back(jnp.dot(normed, w_qkv[layer_at], precision=HIGH)).reshape(TOKENS, 3, HEADS, HEAD)
        queries = low(low_back(rotate(qkv_rows[:, 0], cosine, sine_tab)))
        key_rows = low(low_back(rotate(qkv_rows[:, 1], cosine, sine_tab)))
        values = low(low_back(qkv_rows[:, 2]))
        mixture = attention(queries, key_rows, values, doc_all, reach)
        mixture = low(low_back(mixture.reshape(TOKENS, D)))
        stream = stream + low_back(jnp.dot(mixture, w_attn_out[layer_at], precision=HIGH))
        normed_ff = low(layer_norm(stream, gains[layer_at, 1]))
        lifted = low_back(jnp.dot(normed_ff, w_in[layer_at], precision=HIGH))
        gated_act = low(jax.nn.gelu(lifted[:, :FF], approximate=False) * lifted[:, FF:])
        stream = stream + low_back(jnp.dot(gated_act, w_ff_out[layer_at], precision=HIGH))
    return stream

def reference(hidden_in, cu_lengths, w_qkv, w_attn_out, w_in, w_ff_out, gains, cotangent):

    def run(stream, first, second, third, fourth, scales):
        return forward(stream, first, second, third, fourth, scales, cu_lengths)
    inputs = [arr.astype(jnp.float32) for arr in (hidden_in, w_qkv, w_attn_out, w_in, w_ff_out, gains)]
    result, pullback = jax.vjp(run, *inputs)
    grads = pullback(cotangent.astype(jnp.float32))
    return (result.astype(jnp.bfloat16), grads[0], grads[1], grads[2], grads[3], grads[4], grads[5])
```

```python
import functools

import jax
import jax.numpy as jnp
from jax import lax
from jax.experimental import pallas as pl
from jax.experimental.pallas import tpu as pltpu
from jax.sharding import PartitionSpec as P

D = 768
HEADS = 12
HEAD = 64
FF = 1152
LAYERS = 2
HALF_WINDOW = 64


EPS = 1e-05
NEG = -1e30
LOCAL_BASE = 10000.0
GLOBAL_BASE = 160000.0


def layer_norm(stream, gain):
    mean_row = jnp.mean(stream, axis=-1, keepdims=True)
    centred = stream - mean_row
    spread = jnp.mean(centred * centred, axis=-1, keepdims=True)
    return centred * lax.rsqrt(spread + EPS) * gain


def geglu(lifted):
    half_width = lifted.shape[-1] // 2
    return jax.nn.gelu(lifted[:, :half_width], approximate=False) * lifted[:, half_width:]


def doc_layout(cu_row, group_rows):
    places = jnp.arange(group_rows, dtype=jnp.int32)
    inner_cuts = cu_row[1:-1]
    doc_ids = jnp.sum((places[:, None] >= inner_cuts[None, :]).astype(jnp.int32), axis=1)
    heads_of = cu_row[:-1]
    starts = jnp.max(jnp.where(places[:, None] >= heads_of[None, :], heads_of[None, :], 0), axis=1)
    return (doc_ids, places - starts)


def rope_tables(positions, base_freq):
    freqs = base_freq ** (-jnp.arange(0, HEAD, 2, dtype=jnp.float32) / HEAD)
    angles = positions.astype(jnp.float32)[:, None] * freqs[None, :]
    angles = jnp.concatenate([angles, angles], axis=1)
    return (jnp.cos(angles), jnp.sin(angles))


def meet_peers(me, count):
    barrier = pltpu.get_barrier_semaphore()
    for step in range(1, count):
        pl.semaphore_signal(
            barrier,
            inc=1,
            device_id={"seq": lax.rem(me + step, count)},
            device_id_type=pl.DeviceIdType.MESH,
        )
    pl.semaphore_wait(barrier, count - 1)


def swap_body(count, same, add, own_ref, out_ref, *scratch):
    if add:
        land_ref, send_sem, recv_sem = scratch
    else:
        send_sem, recv_sem = scratch
        land_ref = out_ref
    me = lax.axis_index("seq")
    meet_peers(me, count)
    copies = []
    for step in range(1, count):
        peer = lax.rem(me + step, count)
        copy = pltpu.make_async_remote_copy(
            src_ref=own_ref if same else own_ref.at[peer],
            dst_ref=land_ref.at[me],
            send_sem=send_sem.at[step - 1],
            recv_sem=recv_sem.at[step - 1],
            device_id={"seq": peer},
            device_id_type=pl.DeviceIdType.MESH,
        )
        copy.start()
        copies.append(copy)
    land_ref[me] = own_ref[...] if same else own_ref[me]
    for copy in copies:
        copy.wait()
    if add:
        total = land_ref[0].astype(jnp.float32)
        for at in range(1, count):
            total = total + land_ref[at].astype(jnp.float32)
        out_ref[...] = total


def swap(blocks, call_id, same=False, add=False):
    count = lax.axis_size("seq")
    piece = blocks.shape if same else blocks.shape[1:]
    out = jax.ShapeDtypeStruct(piece, jnp.float32)
    land = [pltpu.VMEM((count,) + piece, blocks.dtype)]
    if not add:
        out = jax.ShapeDtypeStruct((count,) + piece, blocks.dtype)
        land = []
    return pl.pallas_call(
        functools.partial(swap_body, count, same, add),
        out_shape=out,
        in_specs=[pl.BlockSpec(memory_space=pltpu.VMEM)],
        out_specs=pl.BlockSpec(memory_space=pltpu.VMEM),
        scratch_shapes=land
        + [pltpu.SemaphoreType.DMA((count - 1,)), pltpu.SemaphoreType.DMA((count - 1,))],
        compiler_params=pltpu.CompilerParams(
            collective_id=call_id, has_side_effects=True, vmem_limit_bytes=16 * 2**20
        ),
    )(blocks)


def gather_group(rows):
    return swap(rows, 0, same=True).reshape(-1, rows.shape[1])


def scatter_group(partial):
    count = lax.axis_size("seq")
    rows = partial.astype(jnp.bfloat16).reshape(count, -1, partial.shape[1])
    return swap(rows, 1, add=True)


def dot(left, right):
    return jnp.dot(left, right, preferred_element_type=jnp.float32)


def dot_t(left, right):
    return lax.dot_general(left, right, (((1,), (1,)), ((), ())), preferred_element_type=jnp.float32)


def t_dot(left, right):
    return lax.dot_general(left, right, (((0,), (0,)), ((), ())), preferred_element_type=jnp.float32)


def turn(values, cosine, sine_tab):
    half_width = HEAD // 2
    turned = jnp.concatenate([-values[..., half_width:], values[..., :half_width]], axis=-1)
    return values * cosine + turned * sine_tab


def turn_back(gradient, cosine, sine_tab):
    half_width = HEAD // 2
    scaled = gradient * sine_tab
    turned = jnp.concatenate([scaled[..., half_width:], -scaled[..., :half_width]], axis=-1)
    return gradient * cosine + turned


def on_device(hidden_in, cu_lengths, w_qkv, w_attn_out, w_in, w_ff_out, gains, cotangent):
    local_rows = hidden_in.shape[0]
    seq_count = lax.axis_size("seq")
    seq_at = lax.axis_index("seq")
    shards = lax.axis_size("fsdp")
    group_rows = local_rows * seq_count
    part_width = D // seq_count
    part_heads = part_width // HEAD
    part_ff = FF // seq_count
    ff_rows = w_ff_out.shape[1]
    spread_ff = ff_rows % seq_count == 0
    scale = HEAD**-0.5

    doc_ids, positions = doc_layout(cu_lengths[0], group_rows)
    places = jnp.arange(group_rows, dtype=jnp.int32)
    same_doc = doc_ids[:, None] == doc_ids[None, :]
    distance = jnp.abs(places[:, None] - places[None, :])

    def own_columns(weight):
        cut = weight.reshape(LAYERS, weight.shape[1], 3, seq_count, part_width)
        return lax.dynamic_index_in_dim(cut, seq_at, 3, keepdims=False).reshape(
            LAYERS, weight.shape[1], 3 * part_width
        )

    qkv_cut = own_columns(w_qkv)
    if spread_ff:
        unit = ff_rows // seq_count
        cut = w_in.reshape(LAYERS, w_in.shape[1], 2, shards, seq_count, unit)
        lift_cut = lax.dynamic_index_in_dim(cut, seq_at, 4, keepdims=False)
        down_cut = lax.dynamic_slice_in_dim(w_ff_out, seq_at * unit, unit, 1)
    else:
        cut = w_in.reshape(LAYERS, w_in.shape[1], 2, seq_count, part_ff)
        lift_cut = lax.dynamic_index_in_dim(cut, seq_at, 3, keepdims=False)
        down_cut = w_ff_out
    lift_cut = lift_cut.reshape(LAYERS, w_in.shape[1], 2 * part_ff)
    gain_cut = gains.reshape(LAYERS * 2, -1).T

    def collect(shard):
        return lax.all_gather(shard, "fsdp", axis=0, tiled=True)

    weights = []
    for layer_at in range(LAYERS):
        first = [qkv_cut[layer_at]]
        if layer_at == 0:
            first.append(gain_cut)
        rest = jnp.concatenate([w_attn_out[layer_at], lift_cut[layer_at]], axis=1)
        first = collect(jnp.concatenate(first, axis=1))
        rest = collect(rest)
        down = collect(down_cut[layer_at])
        if not spread_ff:
            down = lax.dynamic_slice_in_dim(down, seq_at * part_ff, part_ff, 0)
        if layer_at == 0:
            gain_full = first[:, 3 * part_width :].T.astype(jnp.float32)
        weights.append((first[:, : 3 * part_width], rest[:, :D], rest[:, D:], down))
    gain_full = gain_full.reshape(LAYERS, 2, 1, D)

    stream = hidden_in.astype(jnp.float32)
    stored = []
    for layer_at in range(LAYERS):
        qkv_w, proj_w, lift_w, down_w = weights[layer_at]
        reach = HALF_WINDOW if layer_at == 0 else group_rows
        base_freq = LOCAL_BASE if layer_at == 0 else GLOBAL_BASE
        cosine, sine_tab = rope_tables(positions, base_freq)
        allowed = same_doc & (distance <= reach)
        entering = stream
        normed = layer_norm(stream, gain_full[layer_at, 0]).astype(jnp.bfloat16)
        normed_all = gather_group(normed)
        qkv = dot(normed_all, qkv_w)
        qkv = qkv.reshape(group_rows, 3, part_heads, HEAD).transpose(1, 2, 0, 3)
        q = turn(qkv[0], cosine, sine_tab).astype(jnp.bfloat16)
        k = turn(qkv[1], cosine, sine_tab).astype(jnp.bfloat16)
        v = qkv[2].astype(jnp.bfloat16)
        scores = jnp.einsum("hqd,hkd->hqk", q, k, preferred_element_type=jnp.float32) * scale
        scores = jnp.where(allowed[None], scores, NEG)
        expd = jnp.exp(scores - jnp.max(scores, axis=-1, keepdims=True))
        probs = expd / jnp.sum(expd, axis=-1, keepdims=True)
        mixture = jnp.einsum(
            "hqk,hkd->qhd", probs.astype(jnp.bfloat16), v, preferred_element_type=jnp.float32
        )
        mixture = mixture.astype(jnp.bfloat16).reshape(group_rows, part_width)
        mix_all = swap(mixture, 2, same=True)
        returned = lax.dynamic_slice_in_dim(mix_all, seq_at * local_rows, local_rows, 1)
        returned = returned.transpose(1, 0, 2).reshape(local_rows, D)
        stream = stream + dot(returned, proj_w)
        middle = stream
        normed_ff = layer_norm(stream, gain_full[layer_at, 1]).astype(jnp.bfloat16)
        normed_ff_all = gather_group(normed_ff)
        lifted = dot(normed_ff_all, lift_w)
        gated = geglu(lifted).astype(jnp.bfloat16)
        stream = stream + scatter_group(dot(gated, down_w))
        stored.append(
            (
                entering,
                normed_all,
                q,
                k,
                v,
                probs,
                allowed,
                cosine,
                sine_tab,
                mix_all,
                middle,
                normed_ff_all,
                lifted,
                gated,
            )
        )
    block_out = stream.astype(jnp.bfloat16)
    gradient = cotangent.astype(jnp.float32)
    grads = [None] * LAYERS
    for layer_at in reversed(range(LAYERS)):
        (
            entering,
            normed_all,
            q,
            k,
            v,
            probs,
            allowed,
            cosine,
            sine_tab,
            mix_all,
            middle,
            normed_ff_all,
            lifted,
            gated,
        ) = stored[layer_at]
        qkv_w, proj_w, lift_w, down_w = weights[layer_at]
        grad_y = gather_group(gradient.astype(jnp.bfloat16))
        _, pullback = jax.vjp(geglu, lifted)
        grad_lift = pullback(dot_t(grad_y, down_w))[0].astype(jnp.bfloat16)
        grad_normed = scatter_group(dot_t(grad_lift, lift_w))
        _, pullback = jax.vjp(layer_norm, middle, gain_full[layer_at, 1])
        grad_input, gain_ffn = pullback(grad_normed)
        gradient = gradient + grad_input
        grad_a = gradient.astype(jnp.bfloat16)
        grad_mix = dot_t(grad_a, proj_w).astype(jnp.bfloat16)
        pair = jnp.stack(
            [
                grad_mix.reshape(local_rows, seq_count, part_width),
                grad_a.reshape(local_rows, seq_count, part_width),
            ]
        ).transpose(2, 0, 1, 3)
        pair = swap(pair, 3)
        grad_heads = (
            pair[:, 0].reshape(group_rows, part_heads, HEAD).transpose(1, 0, 2)
        )
        grad_a_part = pair[:, 1].reshape(group_rows, part_width)
        grad_probs = jnp.einsum("hqd,hkd->hqk", grad_heads, v, preferred_element_type=jnp.float32)
        centre = jnp.sum(probs * grad_probs, axis=-1, keepdims=True)
        grad_scores = (probs * (grad_probs - centre)).astype(jnp.bfloat16)
        grad_q = jnp.einsum("hqk,hkd->hqd", grad_scores, k, preferred_element_type=jnp.float32)
        grad_k = jnp.einsum("hqk,hqd->hkd", grad_scores, q, preferred_element_type=jnp.float32)
        grad_v = jnp.einsum(
            "hqk,hqd->hkd",
            probs.astype(jnp.bfloat16),
            grad_heads,
            preferred_element_type=jnp.float32,
        )
        grad_qkv = jnp.stack(
            [
                turn_back(grad_q * scale, cosine, sine_tab),
                turn_back(grad_k * scale, cosine, sine_tab),
                grad_v,
            ]
        ).astype(jnp.bfloat16)
        grad_qkv = grad_qkv.transpose(2, 0, 1, 3).reshape(group_rows, 3 * part_width)
        grad_normed = scatter_group(dot_t(grad_qkv, qkv_w))
        _, pullback = jax.vjp(layer_norm, entering, gain_full[layer_at, 0])
        grad_input, gain_attn = pullback(grad_normed)
        gradient = gradient + grad_input

        proj_grad = lax.dot_general(
            mix_all,
            grad_a_part,
            (((1,), (0,)), ((), ())),
            preferred_element_type=jnp.float32,
        ).reshape(D, part_width)
        early = jnp.concatenate(
            [t_dot(normed_ff_all, grad_lift), proj_grad], axis=1
        ).astype(jnp.bfloat16)
        late = jnp.concatenate(
            [t_dot(normed_all, grad_qkv), gain_attn.T, gain_ffn.T], axis=1
        ).astype(jnp.bfloat16)
        down_grad = t_dot(gated, grad_y).astype(jnp.bfloat16)
        if not spread_ff:
            wide = jnp.zeros((FF, D), jnp.bfloat16)
            down_grad = lax.dynamic_update_slice_in_dim(wide, down_grad, seq_at * part_ff, 0)
        sums = [
            lax.psum_scatter(part, "fsdp", scatter_dimension=0, tiled=True)
            for part in (down_grad, early, late)
        ]
        grads[layer_at] = [
            lax.all_gather(part, "seq", axis=0, tiled=False).astype(jnp.float32) for part in sums
        ]

    def whole(parts, blocks, width):
        parts = parts.reshape(seq_count, -1, blocks, width)
        return parts.transpose(1, 2, 0, 3).reshape(parts.shape[1], blocks * seq_count * width)

    out = [[], [], [], [], []]
    for down, early, late in grads:
        out[0].append(whole(late[:, :, : 3 * part_width], 3, part_width))
        out[1].append(whole(early[:, :, 2 * part_ff :], 1, part_width))
        lift = early[:, :, : 2 * part_ff]
        if spread_ff:
            out[2].append(whole(lift, 2 * shards, ff_rows // seq_count))
            out[3].append(down.reshape(ff_rows, D))
        else:
            out[2].append(whole(lift, 2, part_ff))
            out[3].append(jnp.sum(down, axis=0))
        out[4].append(jnp.sum(late[:, :, 3 * part_width :], axis=0).T)
    return (block_out, gradient, *[jnp.stack(member) for member in out])


def solution(mesh):
    return jax.shard_map(
        on_device,
        mesh=mesh,
        in_specs=(
            P(("fsdp", "seq"), None),
            P("fsdp", None),
            P(None, "fsdp", None),
            P(None, "fsdp", None),
            P(None, "fsdp", None),
            P(None, "fsdp", None),
            P(None, None, "fsdp"),
            P(("fsdp", "seq"), None),
        ),
        out_specs=(
            P(("fsdp", "seq"), None),
            P(("fsdp", "seq"), None),
            P(None, "fsdp", None),
            P(None, "fsdp", None),
            P(None, "fsdp", None),
            P(None, "fsdp", None),
            P(None, None, "fsdp"),
        ),
        check_vma=False,
    )
```

```python
import functools

import jax
import jax.numpy as jnp
from jax import lax
from jax.experimental import pallas as pl
from jax.experimental.pallas import tpu as pltpu
from jax.sharding import PartitionSpec as P

D = 768
HEADS = 12
HEAD = 64
FF = 1152
LAYERS = 2
HALF_WINDOW = 64


EPS = 1e-05
NEG = -1e30
LOCAL_BASE = 10000.0
GLOBAL_BASE = 160000.0


def layer_norm(stream, gain):
    mean_row = jnp.mean(stream, axis=-1, keepdims=True)
    centred = stream - mean_row
    spread = jnp.mean(centred * centred, axis=-1, keepdims=True)
    return centred * lax.rsqrt(spread + EPS) * gain


def geglu(lifted):
    half_width = lifted.shape[-1] // 2
    return jax.nn.gelu(lifted[:, :half_width], approximate=False) * lifted[:, half_width:]


def doc_layout(cu_row, group_rows):
    places = jnp.arange(group_rows, dtype=jnp.int32)
    inner_cuts = cu_row[1:-1]
    doc_ids = jnp.sum((places[:, None] >= inner_cuts[None, :]).astype(jnp.int32), axis=1)
    heads_of = cu_row[:-1]
    starts = jnp.max(jnp.where(places[:, None] >= heads_of[None, :], heads_of[None, :], 0), axis=1)
    return (doc_ids, places - starts)


def rope_tables(positions, base_freq):
    freqs = base_freq ** (-jnp.arange(0, HEAD, 2, dtype=jnp.float32) / HEAD)
    angles = positions.astype(jnp.float32)[:, None] * freqs[None, :]
    angles = jnp.concatenate([angles, angles], axis=1)
    return (jnp.cos(angles), jnp.sin(angles))


MESH = pl.DeviceIdType.MESH


def meet(axis, peers):
    barrier = pltpu.get_barrier_semaphore()
    for peer in peers:
        pl.semaphore_signal(barrier, inc=1, device_id={axis: peer}, device_id_type=MESH)
    pl.semaphore_wait(barrier, len(peers))


def push(axis, peer, source, target, sems, at):
    copy = pltpu.make_async_remote_copy(
        src_ref=source,
        dst_ref=target,
        send_sem=sems.at[0, at],
        recv_sem=sems.at[1, at],
        device_id={axis: peer},
        device_id_type=MESH,
    )
    copy.start()
    return copy


def chip_peers():
    me = lax.axis_index("seq")
    chip, core = me // 2, me % 2
    return me, 2 * chip + 1 - core, 2 * (1 - chip) + core, 2 * (1 - chip) + 1 - core


def spread_body(own_ref, out_ref, sems):
    me, sibling, across, _ = chip_peers()
    meet("seq", (sibling, across))
    far = push("seq", across, own_ref, out_ref.at[me], sems, 0)
    near = push("seq", sibling, own_ref, out_ref.at[me], sems, 1)
    out_ref[me] = own_ref[...]
    far.wait_recv()
    onward = push("seq", sibling, out_ref.at[across], out_ref.at[across], sems, 2)
    far.wait_send()
    near.wait()
    onward.wait()


def fold_body(own_ref, out_ref, land, passing, arrived, sems):
    me, sibling, across, diagonal = chip_peers()
    meet("seq", (sibling, across))
    first = push("seq", sibling, own_ref.at[diagonal], land.at[0], sems, 0)
    second = push("seq", sibling, own_ref.at[sibling], land.at[1], sems, 1)
    first.wait_recv()
    total = own_ref[across].astype(jnp.float32) + land[0].astype(jnp.float32)
    passing[...] = total.astype(passing.dtype)
    third = push("seq", across, passing, arrived, sems, 2)
    second.wait_recv()
    mine = own_ref[me].astype(jnp.float32) + land[1].astype(jnp.float32)
    third.wait_recv()
    out_ref[...] = mine + arrived[...].astype(jnp.float32)
    first.wait_send()
    second.wait_send()
    third.wait_send()


def trade_body(count, own_ref, out_ref, sems):
    me = lax.axis_index("seq")
    peers = [lax.rem(me + step, count) for step in range(1, count)]
    meet("seq", peers)
    copies = [
        push("seq", peer, own_ref.at[peer], out_ref.at[me], sems, at)
        for at, peer in enumerate(peers)
    ]
    out_ref[me] = own_ref[me]
    for copy in copies:
        copy.wait()


def call(body, out, scratch, call_id, *operands):
    space = pl.BlockSpec(memory_space=pltpu.VMEM)
    many = isinstance(out, list)
    return pl.pallas_call(
        body,
        out_shape=out,
        in_specs=[space] * len(operands),
        out_specs=[space] * len(out) if many else space,
        scratch_shapes=scratch,
        compiler_params=pltpu.CompilerParams(
            collective_id=call_id, has_side_effects=True, vmem_limit_bytes=40 * 2**20
        ),
    )(*operands)


def pair_sems(*shape):
    return pltpu.SemaphoreType.DMA((2,) + shape)


def spread(rows, call_id):
    out = jax.ShapeDtypeStruct((4,) + rows.shape, rows.dtype)
    return call(spread_body, out, [pair_sems(3)], call_id, rows)


def fold(blocks, call_id):
    piece = blocks.shape[1:]
    out = jax.ShapeDtypeStruct(piece, jnp.float32)
    scratch = [pltpu.VMEM(shape, blocks.dtype) for shape in ((2,) + piece, piece, piece)]
    return call(fold_body, out, scratch + [pair_sems(3)], call_id, blocks)


def trade(blocks, call_id):
    count = blocks.shape[0]
    out = jax.ShapeDtypeStruct(blocks.shape, blocks.dtype)
    return call(functools.partial(trade_body, count), out, [pair_sems(count - 1)], call_id, blocks)


def plane_peers(deep):
    me = lax.axis_index("fsdp")
    z, y = me // 2, me % 2
    beside = 2 * z + 1 - y
    ahead = [2 * ((z + step) % deep) + y for step in range(1, deep)]
    behind = [2 * ((z + deep - step) % deep) + y for step in range(1, deep)]
    return me, z, y, beside, ahead, behind


def collect_body(arrays, deep, *refs):
    owns, outs = refs[:arrays], refs[arrays : 2 * arrays]
    sems = refs[2 * arrays]
    me, z, y, beside, ahead, behind = plane_peers(deep)
    meet("fsdp", [beside] + ahead)
    every = 2 * deep - 1
    along = []
    copies = []
    for at in range(arrays):
        for step, peer in enumerate(ahead):
            along.append(push("fsdp", peer, owns[at], outs[at].at[me], sems, at * every + step))
        near = push("fsdp", beside, owns[at], outs[at].at[me], sems, at * every + deep - 1)
        copies.append(near)
        outs[at][me] = owns[at][...]
    for at in range(arrays):
        for step, origin in enumerate(behind):
            along[at * (deep - 1) + step].wait_recv()
            block = outs[at].at[origin]
            copies.append(push("fsdp", beside, block, block, sems, at * every + deep + step))
    for copy in along:
        copy.wait_send()
    for copy in copies:
        copy.wait()


def collect_all(owns, shards):
    out = [jax.ShapeDtypeStruct((shards,) + own.shape, own.dtype) for own in owns]
    deep = shards // 2
    sems = pair_sems(len(owns) * (2 * deep - 1))
    return call(functools.partial(collect_body, len(owns), deep), out, [sems], 5, *owns)


def reduce_body(arrays, deep, *refs):
    parts, outs = refs[:arrays], refs[arrays : 2 * arrays]
    lands, arrivals = refs[2 * arrays : 3 * arrays], refs[3 * arrays : 4 * arrays]
    sems = refs[4 * arrays]
    me, z, y, beside, ahead, behind = plane_peers(deep)
    meet("fsdp", [beside] + ahead)
    every = 2 * deep - 1
    near = []
    far = []
    order = list(range(1, deep)) + [0]
    for at in range(arrays):
        for step in order:
            source = parts[at].at[2 * ((z + step) % deep) + 1 - y]
            near.append(push("fsdp", beside, source, lands[at].at[step], sems, at * every + step))
    for at in range(arrays):
        for place, step in enumerate(order):
            near[at * deep + place].wait_recv()
            mine = parts[at][2 * ((z + step) % deep) + y].astype(jnp.float32)
            total = mine + lands[at][step].astype(jnp.float32)
            lands[at][step] = total.astype(jnp.bfloat16)
            if step:
                target = arrivals[at].at[step - 1]
                sem_at = at * every + deep + step - 1
                far.append(push("fsdp", ahead[step - 1], lands[at].at[step], target, sems, sem_at))
    for at in range(arrays):
        total = lands[at][0].astype(jnp.float32)
        for step in range(deep - 1):
            far[at * (deep - 1) + step].wait_recv()
            total = total + arrivals[at][step].astype(jnp.float32)
        outs[at][...] = total.astype(jnp.bfloat16)
    for copy in near + far:
        copy.wait_send()


def reduce_all(parts):
    shards = parts[0].shape[0]
    deep = shards // 2
    pieces = [part.shape[1:] for part in parts]
    out = [jax.ShapeDtypeStruct(piece, jnp.bfloat16) for piece in pieces]
    scratch = [pltpu.VMEM((deep,) + piece, jnp.bfloat16) for piece in pieces]
    scratch += [pltpu.VMEM((deep - 1,) + piece, jnp.bfloat16) for piece in pieces]
    scratch.append(pair_sems(len(parts) * (2 * deep - 1)))
    return call(functools.partial(reduce_body, len(parts), deep), out, scratch, 6, *parts)


def gather_group(rows):
    return spread(rows, 0).reshape(-1, rows.shape[1])


def scatter_group(partial):
    count = lax.axis_size("seq")
    rows = partial.astype(jnp.bfloat16).reshape(count, -1, partial.shape[1])
    return fold(rows, 1)


def dot(left, right):
    return jnp.dot(left, right, preferred_element_type=jnp.float32)


def dot_t(left, right):
    return lax.dot_general(left, right, (((1,), (1,)), ((), ())), preferred_element_type=jnp.float32)


def t_dot(left, right):
    return lax.dot_general(left, right, (((0,), (0,)), ((), ())), preferred_element_type=jnp.float32)


def turn(values, cosine, sine_tab):
    half_width = HEAD // 2
    turned = jnp.concatenate([-values[..., half_width:], values[..., :half_width]], axis=-1)
    return values * cosine + turned * sine_tab


def turn_back(gradient, cosine, sine_tab):
    half_width = HEAD // 2
    scaled = gradient * sine_tab
    turned = jnp.concatenate([scaled[..., half_width:], -scaled[..., :half_width]], axis=-1)
    return gradient * cosine + turned


def on_device(hidden_in, cu_lengths, w_qkv, w_attn_out, w_in, w_ff_out, gains, cotangent):
    local_rows = hidden_in.shape[0]
    seq_count = lax.axis_size("seq")
    seq_at = lax.axis_index("seq")
    shards = lax.axis_size("fsdp")
    group_rows = local_rows * seq_count
    part_width = D // seq_count
    part_heads = part_width // HEAD
    part_ff = FF // seq_count
    ff_rows = w_ff_out.shape[1]
    spread_ff = ff_rows % seq_count == 0
    scale = HEAD**-0.5

    doc_ids, positions = doc_layout(cu_lengths[0], group_rows)
    places = jnp.arange(group_rows, dtype=jnp.int32)
    same_doc = doc_ids[:, None] == doc_ids[None, :]
    distance = jnp.abs(places[:, None] - places[None, :])

    def own_columns(weight):
        cut = weight.reshape(LAYERS, weight.shape[1], 3, seq_count, part_width)
        return lax.dynamic_index_in_dim(cut, seq_at, 3, keepdims=False).reshape(
            LAYERS, weight.shape[1], 3 * part_width
        )

    qkv_cut = own_columns(w_qkv)
    if spread_ff:
        unit = ff_rows // seq_count
        cut = w_in.reshape(LAYERS, w_in.shape[1], 2, shards, seq_count, unit)
        lift_cut = lax.dynamic_index_in_dim(cut, seq_at, 4, keepdims=False)
        down_cut = lax.dynamic_slice_in_dim(w_ff_out, seq_at * unit, unit, 1)
    else:
        cut = w_in.reshape(LAYERS, w_in.shape[1], 2, seq_count, part_ff)
        lift_cut = lax.dynamic_index_in_dim(cut, seq_at, 3, keepdims=False)
        down_cut = w_ff_out
    lift_cut = lift_cut.reshape(LAYERS, w_in.shape[1], 2 * part_ff)
    gain_cut = gains.reshape(LAYERS * 2, -1).T

    def fill(rows, height, width):
        return jnp.pad(rows, ((0, height - rows.shape[0]), (0, width - rows.shape[1])))

    near = shards == 8
    unit_pad = -(-down_cut.shape[1] // 16) * 16 if spread_ff else down_cut.shape[1]
    first_width = 3 * part_width + 64
    owns = []
    for layer_at in range(LAYERS):
        first = qkv_cut[layer_at]
        if layer_at == 0:
            first = jnp.concatenate([first, gain_cut], axis=1)
            first = fill(first, first.shape[0], first_width)
        owns.append(first)
        owns.append(jnp.concatenate([w_attn_out[layer_at], lift_cut[layer_at]], axis=1))
        owns.append(fill(down_cut[layer_at], unit_pad, D))
    if near:
        full = collect_all(owns, shards)
    else:
        full = [lax.all_gather(own, "fsdp", axis=0, tiled=False) for own in owns]
    weights = []
    for layer_at in range(LAYERS):
        first, rest, down = full[3 * layer_at : 3 * layer_at + 3]
        first = first.reshape(D, -1)
        rest = rest.reshape(D, -1)
        if spread_ff:
            down = down[:, :unit].reshape(part_ff, D)
        else:
            down = lax.dynamic_slice_in_dim(down.reshape(FF, D), seq_at * part_ff, part_ff, 0)
        if layer_at == 0:
            gain_full = first[:, 3 * part_width : 3 * part_width + 4].T.astype(jnp.float32)
        weights.append((first[:, : 3 * part_width], rest[:, :D], rest[:, D:], down))
    gain_full = gain_full.reshape(LAYERS, 2, 1, D)

    stream = hidden_in.astype(jnp.float32)
    stored = []
    for layer_at in range(LAYERS):
        qkv_w, proj_w, lift_w, down_w = weights[layer_at]
        reach = HALF_WINDOW if layer_at == 0 else group_rows
        base_freq = LOCAL_BASE if layer_at == 0 else GLOBAL_BASE
        cosine, sine_tab = rope_tables(positions, base_freq)
        allowed = same_doc & (distance <= reach)
        entering = stream
        normed = layer_norm(stream, gain_full[layer_at, 0]).astype(jnp.bfloat16)
        normed_all = gather_group(normed)
        qkv = dot(normed_all, qkv_w)
        qkv = qkv.reshape(group_rows, 3, part_heads, HEAD).transpose(1, 2, 0, 3)
        q = turn(qkv[0], cosine, sine_tab).astype(jnp.bfloat16)
        k = turn(qkv[1], cosine, sine_tab).astype(jnp.bfloat16)
        v = qkv[2].astype(jnp.bfloat16)
        scores = jnp.einsum("hqd,hkd->hqk", q, k, preferred_element_type=jnp.float32) * scale
        scores = jnp.where(allowed[None], scores, NEG)
        expd = jnp.exp(scores - jnp.max(scores, axis=-1, keepdims=True))
        probs = expd / jnp.sum(expd, axis=-1, keepdims=True)
        mixture = jnp.einsum(
            "hqk,hkd->qhd", probs.astype(jnp.bfloat16), v, preferred_element_type=jnp.float32
        )
        mixture = mixture.astype(jnp.bfloat16).reshape(group_rows, part_width)
        mix_all = spread(mixture, 2)
        returned = lax.dynamic_slice_in_dim(mix_all, seq_at * local_rows, local_rows, 1)
        returned = returned.transpose(1, 0, 2).reshape(local_rows, D)
        stream = stream + dot(returned, proj_w)
        middle = stream
        normed_ff = layer_norm(stream, gain_full[layer_at, 1]).astype(jnp.bfloat16)
        normed_ff_all = gather_group(normed_ff)
        lifted = dot(normed_ff_all, lift_w)
        gated = geglu(lifted).astype(jnp.bfloat16)
        stream = stream + scatter_group(dot(gated, down_w))
        stored.append(
            (
                entering,
                normed_all,
                q,
                k,
                v,
                probs,
                allowed,
                cosine,
                sine_tab,
                mix_all,
                middle,
                normed_ff_all,
                lifted,
                gated,
            )
        )
    block_out = stream.astype(jnp.bfloat16)
    gradient = cotangent.astype(jnp.float32)
    grads = [None] * LAYERS
    for layer_at in reversed(range(LAYERS)):
        (
            entering,
            normed_all,
            q,
            k,
            v,
            probs,
            allowed,
            cosine,
            sine_tab,
            mix_all,
            middle,
            normed_ff_all,
            lifted,
            gated,
        ) = stored[layer_at]
        qkv_w, proj_w, lift_w, down_w = weights[layer_at]
        grad_y = gather_group(gradient.astype(jnp.bfloat16))
        _, pullback = jax.vjp(geglu, lifted)
        grad_lift = pullback(dot_t(grad_y, down_w))[0].astype(jnp.bfloat16)
        grad_normed = scatter_group(dot_t(grad_lift, lift_w))
        _, pullback = jax.vjp(layer_norm, middle, gain_full[layer_at, 1])
        grad_input, gain_ffn = pullback(grad_normed)
        gradient = gradient + grad_input
        grad_a = gradient.astype(jnp.bfloat16)
        grad_mix = dot_t(grad_a, proj_w).astype(jnp.bfloat16)
        pair = jnp.stack(
            [
                grad_mix.reshape(local_rows, seq_count, part_width),
                grad_a.reshape(local_rows, seq_count, part_width),
            ]
        ).transpose(2, 0, 1, 3)
        pair = trade(pair, 3)
        grad_heads = (
            pair[:, 0].reshape(group_rows, part_heads, HEAD).transpose(1, 0, 2)
        )
        grad_a_part = pair[:, 1].reshape(group_rows, part_width)
        grad_probs = jnp.einsum("hqd,hkd->hqk", grad_heads, v, preferred_element_type=jnp.float32)
        centre = jnp.sum(probs * grad_probs, axis=-1, keepdims=True)
        grad_scores = (probs * (grad_probs - centre)).astype(jnp.bfloat16)
        grad_q = jnp.einsum("hqk,hkd->hqd", grad_scores, k, preferred_element_type=jnp.float32)
        grad_k = jnp.einsum("hqk,hqd->hkd", grad_scores, q, preferred_element_type=jnp.float32)
        grad_v = jnp.einsum(
            "hqk,hqd->hkd",
            probs.astype(jnp.bfloat16),
            grad_heads,
            preferred_element_type=jnp.float32,
        )
        grad_qkv = jnp.stack(
            [
                turn_back(grad_q * scale, cosine, sine_tab),
                turn_back(grad_k * scale, cosine, sine_tab),
                grad_v,
            ]
        ).astype(jnp.bfloat16)
        grad_qkv = grad_qkv.transpose(2, 0, 1, 3).reshape(group_rows, 3 * part_width)
        grad_normed = scatter_group(dot_t(grad_qkv, qkv_w))
        _, pullback = jax.vjp(layer_norm, entering, gain_full[layer_at, 0])
        grad_input, gain_attn = pullback(grad_normed)
        gradient = gradient + grad_input

        proj_grad = lax.dot_general(
            mix_all,
            grad_a_part,
            (((1,), (0,)), ((), ())),
            preferred_element_type=jnp.float32,
        ).reshape(D, part_width)
        early = jnp.concatenate(
            [t_dot(normed_ff_all, grad_lift), proj_grad], axis=1
        ).astype(jnp.bfloat16)
        late = jnp.concatenate(
            [t_dot(normed_all, grad_qkv), gain_attn.T, gain_ffn.T], axis=1
        ).astype(jnp.bfloat16)
        late = fill(late, D, first_width)
        down_grad = t_dot(gated, grad_y).astype(jnp.bfloat16)
        if spread_ff:
            down_grad = jnp.pad(
                down_grad.reshape(shards, unit, D), ((0, 0), (0, unit_pad - unit), (0, 0))
            )
        else:
            wide = jnp.zeros((FF, D), jnp.bfloat16)
            down_grad = lax.dynamic_update_slice_in_dim(wide, down_grad, seq_at * part_ff, 0)
            down_grad = down_grad.reshape(shards, -1, D)
        grads[layer_at] = [
            down_grad,
            early.reshape(shards, -1, D),
            late.reshape(shards, -1, first_width),
        ]

    parts = grads[1] + grads[0]
    if near:
        sums = reduce_all(parts)
    else:
        sums = [lax.psum_scatter(part, "fsdp", scatter_dimension=0) for part in parts]
    sums = [jnp.concatenate([sums[at + 3], sums[at]], axis=0) for at in range(3)]
    sums = [spread(part, 7 + at).astype(jnp.float32) for at, part in enumerate(sums)]
    sums = [part.reshape(seq_count, LAYERS, -1, part.shape[-1]) for part in sums]
    grads = [[part[:, layer_at] for part in sums] for layer_at in range(LAYERS)]

    def whole(parts, blocks, width):
        parts = parts.reshape(seq_count, -1, blocks, width)
        return parts.transpose(1, 2, 0, 3).reshape(parts.shape[1], blocks * seq_count * width)

    out = [[], [], [], [], []]
    for down, early, late in grads:
        out[0].append(whole(late[:, :, : 3 * part_width], 3, part_width))
        out[1].append(whole(early[:, :, 2 * part_ff :], 1, part_width))
        lift = early[:, :, : 2 * part_ff]
        if spread_ff:
            out[2].append(whole(lift, 2 * shards, ff_rows // seq_count))
            out[3].append(down[:, :unit].reshape(ff_rows, D))
        else:
            out[2].append(whole(lift, 2, part_ff))
            out[3].append(jnp.sum(down, axis=0))
        out[4].append(jnp.sum(late[:, :, 3 * part_width : 3 * part_width + 2], axis=0).T)
    return (block_out, gradient, *[jnp.stack(member) for member in out])


def solution(mesh):
    return jax.shard_map(
        on_device,
        mesh=mesh,
        in_specs=(
            P(("fsdp", "seq"), None),
            P("fsdp", None),
            P(None, "fsdp", None),
            P(None, "fsdp", None),
            P(None, "fsdp", None),
            P(None, "fsdp", None),
            P(None, None, "fsdp"),
            P(("fsdp", "seq"), None),
        ),
        out_specs=(
            P(("fsdp", "seq"), None),
            P(("fsdp", "seq"), None),
            P(None, "fsdp", None),
            P(None, "fsdp", None),
            P(None, "fsdp", None),
            P(None, "fsdp", None),
            P(None, None, "fsdp"),
        ),
        check_vma=False,
    )
```

```python
import functools

import jax
import jax.numpy as jnp
from jax import lax
from jax.experimental import pallas as pl
from jax.experimental.pallas import tpu as pltpu
from jax.sharding import PartitionSpec as P

D = 768
HEADS = 12
HEAD = 64
FF = 1152
LAYERS = 2
HALF_WINDOW = 64


EPS = 1e-05
NEG = -1e30
LOCAL_BASE = 10000.0
GLOBAL_BASE = 160000.0


def layer_norm(stream, gain):
    mean_row = jnp.mean(stream, axis=-1, keepdims=True)
    centred = stream - mean_row
    spread = jnp.mean(centred * centred, axis=-1, keepdims=True)
    return centred * lax.rsqrt(spread + EPS) * gain


def geglu(lifted):
    half_width = lifted.shape[-1] // 2
    return jax.nn.gelu(lifted[:, :half_width], approximate=False) * lifted[:, half_width:]


def doc_layout(cu_row, group_rows):
    places = jnp.arange(group_rows, dtype=jnp.int32)
    inner_cuts = cu_row[1:-1]
    doc_ids = jnp.sum((places[:, None] >= inner_cuts[None, :]).astype(jnp.int32), axis=1)
    heads_of = cu_row[:-1]
    starts = jnp.max(jnp.where(places[:, None] >= heads_of[None, :], heads_of[None, :], 0), axis=1)
    return (doc_ids, places - starts)


def rope_tables(positions, base_freq):
    freqs = base_freq ** (-jnp.arange(0, HEAD, 2, dtype=jnp.float32) / HEAD)
    angles = positions.astype(jnp.float32)[:, None] * freqs[None, :]
    angles = jnp.concatenate([angles, angles], axis=1)
    return (jnp.cos(angles), jnp.sin(angles))


MESH = pl.DeviceIdType.MESH


def meet(axis, peers):
    barrier = pltpu.get_barrier_semaphore()
    for peer in peers:
        pl.semaphore_signal(barrier, inc=1, device_id={axis: peer}, device_id_type=MESH)
    pl.semaphore_wait(barrier, len(peers))


def push(axis, peer, source, target, sems, at):
    copy = pltpu.make_async_remote_copy(
        src_ref=source,
        dst_ref=target,
        send_sem=sems.at[0, at],
        recv_sem=sems.at[1, at],
        device_id={axis: peer},
        device_id_type=MESH,
    )
    copy.start()
    return copy


def chip_peers():
    me = lax.axis_index("seq")
    chip, core = me // 2, me % 2
    return me, 2 * chip + 1 - core, 2 * (1 - chip) + core, 2 * (1 - chip) + 1 - core


def spread_body(own_ref, out_ref, sems):
    me, sibling, across, _ = chip_peers()
    meet("seq", (sibling, across))
    far = push("seq", across, own_ref, out_ref.at[me], sems, 0)
    near = push("seq", sibling, own_ref, out_ref.at[me], sems, 1)
    out_ref[me] = own_ref[...]
    far.wait_recv()
    onward = push("seq", sibling, out_ref.at[across], out_ref.at[across], sems, 2)
    far.wait_send()
    near.wait()
    onward.wait()


def fold_body(own_ref, out_ref, land, passing, arrived, sems):
    me, sibling, across, diagonal = chip_peers()
    meet("seq", (sibling, across))
    first = push("seq", sibling, own_ref.at[diagonal], land.at[0], sems, 0)
    second = push("seq", sibling, own_ref.at[sibling], land.at[1], sems, 1)
    first.wait_recv()
    total = own_ref[across].astype(jnp.float32) + land[0].astype(jnp.float32)
    passing[...] = total.astype(passing.dtype)
    third = push("seq", across, passing, arrived, sems, 2)
    second.wait_recv()
    mine = own_ref[me].astype(jnp.float32) + land[1].astype(jnp.float32)
    third.wait_recv()
    out_ref[...] = mine + arrived[...].astype(jnp.float32)
    first.wait_send()
    second.wait_send()
    third.wait_send()


def trade_body(count, own_ref, out_ref, sems):
    me = lax.axis_index("seq")
    peers = [lax.rem(me + step, count) for step in range(1, count)]
    meet("seq", peers)
    copies = [
        push("seq", peer, own_ref.at[peer], out_ref.at[me], sems, at)
        for at, peer in enumerate(peers)
    ]
    out_ref[me] = own_ref[me]
    for copy in copies:
        copy.wait()


def call(body, out, scratch, call_id, *operands):
    space = pl.BlockSpec(memory_space=pltpu.VMEM)
    many = isinstance(out, list)
    return pl.pallas_call(
        body,
        out_shape=out,
        in_specs=[space] * len(operands),
        out_specs=[space] * len(out) if many else space,
        scratch_shapes=scratch,
        compiler_params=pltpu.CompilerParams(
            collective_id=call_id, has_side_effects=True, vmem_limit_bytes=40 * 2**20
        ),
    )(*operands)


def pair_sems(*shape):
    return pltpu.SemaphoreType.DMA((2,) + shape)


def spread(rows, call_id):
    out = jax.ShapeDtypeStruct((4,) + rows.shape, rows.dtype)
    return call(spread_body, out, [pair_sems(3)], call_id, rows)


def fold(blocks, call_id):
    piece = blocks.shape[1:]
    out = jax.ShapeDtypeStruct(piece, jnp.float32)
    scratch = [pltpu.VMEM(shape, blocks.dtype) for shape in ((2,) + piece, piece, piece)]
    return call(fold_body, out, scratch + [pair_sems(3)], call_id, blocks)


def trade(blocks, call_id):
    count = blocks.shape[0]
    out = jax.ShapeDtypeStruct(blocks.shape, blocks.dtype)
    return call(functools.partial(trade_body, count), out, [pair_sems(count - 1)], call_id, blocks)


def plane_peers(deep):
    me = lax.axis_index("fsdp")
    z, y = me // 2, me % 2
    beside = 2 * z + 1 - y
    ahead = [2 * ((z + step) % deep) + y for step in range(1, deep)]
    behind = [2 * ((z + deep - step) % deep) + y for step in range(1, deep)]
    return me, z, y, beside, ahead, behind


def collect_body(arrays, deep, *refs):
    owns, outs = refs[:arrays], refs[arrays : 2 * arrays]
    sems = refs[2 * arrays]
    me, z, y, beside, ahead, behind = plane_peers(deep)
    meet("fsdp", [beside] + ahead)
    every = 2 * deep - 1
    along = []
    copies = []

    def issue(at):
        for step, peer in enumerate(ahead):
            along.append(push("fsdp", peer, owns[at], outs[at].at[me], sems, at * every + step))
        near = push("fsdp", beside, owns[at], outs[at].at[me], sems, at * every + deep - 1)
        copies.append(near)

    for at in range(min(2, arrays)):
        issue(at)
    for at in range(arrays):
        outs[at][me] = owns[at][...]
        for step, origin in enumerate(behind):
            along[at * (deep - 1) + step].wait_recv()
            block = outs[at].at[origin]
            copies.append(push("fsdp", beside, block, block, sems, at * every + deep + step))
        if at + 2 < arrays:
            issue(at + 2)
    for copy in along:
        copy.wait_send()
    for copy in copies:
        copy.wait()


def collect_all(owns, shards):
    out = [jax.ShapeDtypeStruct((shards,) + own.shape, own.dtype) for own in owns]
    deep = shards // 2
    sems = pair_sems(len(owns) * (2 * deep - 1))
    return call(functools.partial(collect_body, len(owns), deep), out, [sems], 5, *owns)


def reduce_body(arrays, deep, *refs):
    parts, outs = refs[:arrays], refs[arrays : 2 * arrays]
    lands, arrivals = refs[2 * arrays : 3 * arrays], refs[3 * arrays : 4 * arrays]
    sems = refs[4 * arrays]
    me, z, y, beside, ahead, behind = plane_peers(deep)
    meet("fsdp", [beside] + ahead)
    every = 2 * deep - 1
    near = []
    far = []
    order = list(range(1, deep)) + [0]

    def issue(at):
        for step in order:
            source = parts[at].at[2 * ((z + step) % deep) + 1 - y]
            near.append(push("fsdp", beside, source, lands[at].at[step], sems, at * every + step))

    for at in range(min(3, arrays)):
        issue(at)
    for at in range(arrays):
        for place, step in enumerate(order):
            near[at * deep + place].wait_recv()
            mine = parts[at][2 * ((z + step) % deep) + y].astype(jnp.float32)
            total = mine + lands[at][step].astype(jnp.float32)
            lands[at][step] = total.astype(jnp.bfloat16)
            if step:
                target = arrivals[at].at[step - 1]
                sem_at = at * every + deep + step - 1
                far.append(push("fsdp", ahead[step - 1], lands[at].at[step], target, sems, sem_at))
        if at + 3 < arrays:
            issue(at + 3)
    for at in range(arrays):
        total = lands[at][0].astype(jnp.float32)
        for step in range(deep - 1):
            far[at * (deep - 1) + step].wait_recv()
            total = total + arrivals[at][step].astype(jnp.float32)
        outs[at][...] = total.astype(jnp.bfloat16)
    for copy in near + far:
        copy.wait_send()


def reduce_all(parts):
    shards = parts[0].shape[0]
    deep = shards // 2
    pieces = [part.shape[1:] for part in parts]
    out = [jax.ShapeDtypeStruct(piece, jnp.bfloat16) for piece in pieces]
    scratch = [pltpu.VMEM((deep,) + piece, jnp.bfloat16) for piece in pieces]
    scratch += [pltpu.VMEM((deep - 1,) + piece, jnp.bfloat16) for piece in pieces]
    scratch.append(pair_sems(len(parts) * (2 * deep - 1)))
    return call(functools.partial(reduce_body, len(parts), deep), out, scratch, 6, *parts)


def gather_group(rows):
    return spread(rows, 0).reshape(-1, rows.shape[1])


def scatter_group(partial):
    count = lax.axis_size("seq")
    rows = partial.astype(jnp.bfloat16).reshape(count, -1, partial.shape[1])
    return fold(rows, 1)


def dot(left, right):
    return jnp.dot(left, right, preferred_element_type=jnp.float32)


def dot_t(left, right):
    return lax.dot_general(left, right, (((1,), (1,)), ((), ())), preferred_element_type=jnp.float32)


def t_dot(left, right):
    return lax.dot_general(left, right, (((0,), (0,)), ((), ())), preferred_element_type=jnp.float32)


def turn(values, cosine, sine_tab):
    half_width = HEAD // 2
    turned = jnp.concatenate([-values[..., half_width:], values[..., :half_width]], axis=-1)
    return values * cosine + turned * sine_tab


def turn_back(gradient, cosine, sine_tab):
    half_width = HEAD // 2
    scaled = gradient * sine_tab
    turned = jnp.concatenate([scaled[..., half_width:], -scaled[..., :half_width]], axis=-1)
    return gradient * cosine + turned


def on_device(hidden_in, cu_lengths, w_qkv, w_attn_out, w_in, w_ff_out, gains, cotangent):
    local_rows = hidden_in.shape[0]
    seq_count = lax.axis_size("seq")
    seq_at = lax.axis_index("seq")
    shards = lax.axis_size("fsdp")
    group_rows = local_rows * seq_count
    part_width = D // seq_count
    part_heads = part_width // HEAD
    part_ff = FF // seq_count
    ff_rows = w_ff_out.shape[1]
    spread_ff = ff_rows % seq_count == 0
    scale = HEAD**-0.5

    doc_ids, positions = doc_layout(cu_lengths[0], group_rows)
    places = jnp.arange(group_rows, dtype=jnp.int32)
    same_doc = doc_ids[:, None] == doc_ids[None, :]
    distance = jnp.abs(places[:, None] - places[None, :])

    def own_columns(weight):
        cut = weight.reshape(LAYERS, weight.shape[1], 3, seq_count, part_width)
        return lax.dynamic_index_in_dim(cut, seq_at, 3, keepdims=False).reshape(
            LAYERS, weight.shape[1], 3 * part_width
        )

    qkv_cut = own_columns(w_qkv)
    if spread_ff:
        unit = ff_rows // seq_count
        cut = w_in.reshape(LAYERS, w_in.shape[1], 2, shards, seq_count, unit)
        lift_cut = lax.dynamic_index_in_dim(cut, seq_at, 4, keepdims=False)
        down_cut = lax.dynamic_slice_in_dim(w_ff_out, seq_at * unit, unit, 1)
    else:
        cut = w_in.reshape(LAYERS, w_in.shape[1], 2, seq_count, part_ff)
        lift_cut = lax.dynamic_index_in_dim(cut, seq_at, 3, keepdims=False)
        down_cut = w_ff_out
    lift_cut = lift_cut.reshape(LAYERS, w_in.shape[1], 2 * part_ff)
    gain_cut = gains.reshape(LAYERS * 2, -1).T

    def fill(rows, height, width):
        return jnp.pad(rows, ((0, height - rows.shape[0]), (0, width - rows.shape[1])))

    near = shards == 8
    unit_pad = -(-down_cut.shape[1] // 16) * 16 if spread_ff else down_cut.shape[1]
    first_width = 3 * part_width + 64
    owns = []
    for layer_at in range(LAYERS):
        first = qkv_cut[layer_at]
        if layer_at == 0:
            first = jnp.concatenate([first, gain_cut], axis=1)
            first = fill(first, first.shape[0], first_width)
        owns.append(first)
        owns.append(jnp.concatenate([w_attn_out[layer_at], lift_cut[layer_at]], axis=1))
        owns.append(fill(down_cut[layer_at], unit_pad, D))
    if near:
        full = collect_all(owns, shards)
    else:
        full = [lax.all_gather(own, "fsdp", axis=0, tiled=False) for own in owns]
    weights = []
    for layer_at in range(LAYERS):
        first, rest, down = full[3 * layer_at : 3 * layer_at + 3]
        first = first.reshape(D, -1)
        rest = rest.reshape(D, -1)
        if spread_ff:
            down = down[:, :unit].reshape(part_ff, D)
        else:
            down = lax.dynamic_slice_in_dim(down.reshape(FF, D), seq_at * part_ff, part_ff, 0)
        if layer_at == 0:
            gain_full = first[:, 3 * part_width : 3 * part_width + 4].T.astype(jnp.float32)
        weights.append((first[:, : 3 * part_width], rest[:, :D], rest[:, D:], down))
    gain_full = gain_full.reshape(LAYERS, 2, 1, D)

    stream = hidden_in.astype(jnp.float32)
    stored = []
    for layer_at in range(LAYERS):
        qkv_w, proj_w, lift_w, down_w = weights[layer_at]
        reach = HALF_WINDOW if layer_at == 0 else group_rows
        base_freq = LOCAL_BASE if layer_at == 0 else GLOBAL_BASE
        cosine, sine_tab = rope_tables(positions, base_freq)
        allowed = same_doc & (distance <= reach)
        entering = stream
        normed = layer_norm(stream, gain_full[layer_at, 0]).astype(jnp.bfloat16)
        normed_all = gather_group(normed)
        qkv = dot(normed_all, qkv_w)
        qkv = qkv.reshape(group_rows, 3, part_heads, HEAD).transpose(1, 2, 0, 3)
        q = turn(qkv[0], cosine, sine_tab).astype(jnp.bfloat16)
        k = turn(qkv[1], cosine, sine_tab).astype(jnp.bfloat16)
        v = qkv[2].astype(jnp.bfloat16)
        scores = jnp.einsum("hqd,hkd->hqk", q, k, preferred_element_type=jnp.float32) * scale
        scores = jnp.where(allowed[None], scores, NEG)
        expd = jnp.exp(scores - jnp.max(scores, axis=-1, keepdims=True))
        probs = expd / jnp.sum(expd, axis=-1, keepdims=True)
        mixture = jnp.einsum(
            "hqk,hkd->qhd", probs.astype(jnp.bfloat16), v, preferred_element_type=jnp.float32
        )
        mixture = mixture.astype(jnp.bfloat16).reshape(group_rows, part_width)
        mix_all = spread(mixture, 2)
        returned = lax.dynamic_slice_in_dim(mix_all, seq_at * local_rows, local_rows, 1)
        returned = returned.transpose(1, 0, 2).reshape(local_rows, D)
        stream = stream + dot(returned, proj_w)
        middle = stream
        normed_ff = layer_norm(stream, gain_full[layer_at, 1]).astype(jnp.bfloat16)
        normed_ff_all = gather_group(normed_ff)
        lifted = dot(normed_ff_all, lift_w)
        gated = geglu(lifted).astype(jnp.bfloat16)
        stream = stream + scatter_group(dot(gated, down_w))
        stored.append(
            (
                entering,
                normed_all,
                q,
                k,
                v,
                probs,
                allowed,
                cosine,
                sine_tab,
                mix_all,
                middle,
                normed_ff_all,
                lifted,
                gated,
            )
        )
    block_out = stream.astype(jnp.bfloat16)
    gradient = cotangent.astype(jnp.float32)
    grads = [None] * LAYERS
    for layer_at in reversed(range(LAYERS)):
        (
            entering,
            normed_all,
            q,
            k,
            v,
            probs,
            allowed,
            cosine,
            sine_tab,
            mix_all,
            middle,
            normed_ff_all,
            lifted,
            gated,
        ) = stored[layer_at]
        qkv_w, proj_w, lift_w, down_w = weights[layer_at]
        grad_y = gather_group(gradient.astype(jnp.bfloat16))
        _, pullback = jax.vjp(geglu, lifted)
        grad_lift = pullback(dot_t(grad_y, down_w))[0].astype(jnp.bfloat16)
        grad_normed = scatter_group(dot_t(grad_lift, lift_w))
        _, pullback = jax.vjp(layer_norm, middle, gain_full[layer_at, 1])
        grad_input, gain_ffn = pullback(grad_normed)
        gradient = gradient + grad_input
        grad_a = gradient.astype(jnp.bfloat16)
        grad_mix = dot_t(grad_a, proj_w).astype(jnp.bfloat16)
        pair = jnp.stack(
            [
                grad_mix.reshape(local_rows, seq_count, part_width),
                grad_a.reshape(local_rows, seq_count, part_width),
            ]
        ).transpose(2, 0, 1, 3)
        pair = trade(pair, 3)
        grad_heads = (
            pair[:, 0].reshape(group_rows, part_heads, HEAD).transpose(1, 0, 2)
        )
        grad_a_part = pair[:, 1].reshape(group_rows, part_width)
        grad_probs = jnp.einsum("hqd,hkd->hqk", grad_heads, v, preferred_element_type=jnp.float32)
        centre = jnp.sum(probs * grad_probs, axis=-1, keepdims=True)
        grad_scores = (probs * (grad_probs - centre)).astype(jnp.bfloat16)
        grad_q = jnp.einsum("hqk,hkd->hqd", grad_scores, k, preferred_element_type=jnp.float32)
        grad_k = jnp.einsum("hqk,hqd->hkd", grad_scores, q, preferred_element_type=jnp.float32)
        grad_v = jnp.einsum(
            "hqk,hqd->hkd",
            probs.astype(jnp.bfloat16),
            grad_heads,
            preferred_element_type=jnp.float32,
        )
        grad_qkv = jnp.stack(
            [
                turn_back(grad_q * scale, cosine, sine_tab),
                turn_back(grad_k * scale, cosine, sine_tab),
                grad_v,
            ]
        ).astype(jnp.bfloat16)
        grad_qkv = grad_qkv.transpose(2, 0, 1, 3).reshape(group_rows, 3 * part_width)
        grad_normed = scatter_group(dot_t(grad_qkv, qkv_w))
        _, pullback = jax.vjp(layer_norm, entering, gain_full[layer_at, 0])
        grad_input, gain_attn = pullback(grad_normed)
        gradient = gradient + grad_input

        proj_grad = lax.dot_general(
            mix_all,
            grad_a_part,
            (((1,), (0,)), ((), ())),
            preferred_element_type=jnp.float32,
        ).reshape(D, part_width)
        early = jnp.concatenate(
            [t_dot(normed_ff_all, grad_lift), proj_grad], axis=1
        ).astype(jnp.bfloat16)
        late = jnp.concatenate(
            [t_dot(normed_all, grad_qkv), gain_attn.T, gain_ffn.T], axis=1
        ).astype(jnp.bfloat16)
        late = fill(late, D, first_width)
        down_grad = t_dot(gated, grad_y).astype(jnp.bfloat16)
        if spread_ff:
            down_grad = jnp.pad(
                down_grad.reshape(shards, unit, D), ((0, 0), (0, unit_pad - unit), (0, 0))
            )
        else:
            wide = jnp.zeros((FF, D), jnp.bfloat16)
            down_grad = lax.dynamic_update_slice_in_dim(wide, down_grad, seq_at * part_ff, 0)
            down_grad = down_grad.reshape(shards, -1, D)
        grads[layer_at] = [
            down_grad,
            early.reshape(shards, -1, D),
            late.reshape(shards, -1, first_width),
        ]

    parts = grads[1] + grads[0]
    if near:
        sums = reduce_all(parts)
    else:
        sums = [lax.psum_scatter(part, "fsdp", scatter_dimension=0) for part in parts]
    sums = [jnp.concatenate([sums[at + 3], sums[at]], axis=0) for at in range(3)]
    sums = [spread(part, 7 + at).astype(jnp.float32) for at, part in enumerate(sums)]
    sums = [part.reshape(seq_count, LAYERS, -1, part.shape[-1]) for part in sums]
    grads = [[part[:, layer_at] for part in sums] for layer_at in range(LAYERS)]

    def whole(parts, blocks, width):
        parts = parts.reshape(seq_count, -1, blocks, width)
        return parts.transpose(1, 2, 0, 3).reshape(parts.shape[1], blocks * seq_count * width)

    out = [[], [], [], [], []]
    for down, early, late in grads:
        out[0].append(whole(late[:, :, : 3 * part_width], 3, part_width))
        out[1].append(whole(early[:, :, 2 * part_ff :], 1, part_width))
        lift = early[:, :, : 2 * part_ff]
        if spread_ff:
            out[2].append(whole(lift, 2 * shards, ff_rows // seq_count))
            out[3].append(down[:, :unit].reshape(ff_rows, D))
        else:
            out[2].append(whole(lift, 2, part_ff))
            out[3].append(jnp.sum(down, axis=0))
        out[4].append(jnp.sum(late[:, :, 3 * part_width : 3 * part_width + 2], axis=0).T)
    return (block_out, gradient, *[jnp.stack(member) for member in out])


def solution(mesh):
    return jax.shard_map(
        on_device,
        mesh=mesh,
        in_specs=(
            P(("fsdp", "seq"), None),
            P("fsdp", None),
            P(None, "fsdp", None),
            P(None, "fsdp", None),
            P(None, "fsdp", None),
            P(None, "fsdp", None),
            P(None, None, "fsdp"),
            P(("fsdp", "seq"), None),
        ),
        out_specs=(
            P(("fsdp", "seq"), None),
            P(("fsdp", "seq"), None),
            P(None, "fsdp", None),
            P(None, "fsdp", None),
            P(None, "fsdp", None),
            P(None, "fsdp", None),
            P(None, None, "fsdp"),
        ),
        check_vma=False,
    )
```
